32 devices in a mesh: dom: 8 (over z, x), ref: 4 (over y, core).
Axes of the slice: x: 2, y: 2, z: 4, core: 2. Of those that a mesh axis runs over, the one named last changes fastest.
Arguments:
- particles: float32 [1024, 128], P('dom'), may hold values from -1.2 to 1.2
- references: float32 [4096, 128], P('ref'), may hold values from -1 to 1.2
Outputs:
- moved: float32 [1024, 128], P(('dom', 'ref'))
- drift: float32 [1024, 128], P(('dom', 'ref'))
The draws below stay inside these ranges and needn't reach their ends.
All inputs are finite; a program needn't handle non-finite values.
Results may differ from the reference program's by a relative error of at most 0.00035.
Values sent between devices are 32-bit elements; how exact they have to be, the bound alone decides.
No kernel may reach another device: no remote copies, remote signals or barrier semaphores. Data moves between devices by JAX's collectives and lax.ppermute only.
A program may use at most 64 MiB of HBM per device.

```python
import jax
import jax.numpy as jnp
from jax import lax

D = 128
ROWS_DEV = 32
STEPS = 2
NPART = 1024
NREF = 4096
N_REF = 4


wide_count = 4


def wide_columns(key):
    order = jax.random.permutation(jax.random.fold_in(key, 7), D)
    return (order < wide_count).astype(jnp.float32)[None, :]


def draw_particles(key, part):
    column_mask = wide_columns(key)
    first_key, second_key = jax.random.split(jax.random.fold_in(key, 1))
    broad = jax.random.uniform(first_key, (NPART, D), jnp.float32, -1.0, 1.0)
    narrow = 0.08 * jax.random.truncated_normal(second_key, -5.0, 5.0, (NPART, D), jnp.float32)
    return column_mask * broad + (1.0 - column_mask) * narrow


def draw_references(key, part):
    column_mask = wide_columns(key)
    first_key, second_key = jax.random.split(jax.random.fold_in(key, 2))
    broad = jax.random.uniform(first_key, (NREF, D), jnp.float32, -0.8, 1.0)
    narrow = 0.06 * jax.random.truncated_normal(second_key, -5.0, 5.0, (NREF, D), jnp.float32)
    return column_mask * broad + (1.0 - column_mask) * narrow


def setup_inputs(seed: int = 0) -> dict:
    keys = jax.random.split(jax.random.key(seed), 3)
    particles = draw_particles(jax.random.fold_in(keys[2], 71), 0)
    references = draw_references(jax.random.fold_in(keys[2], 71), 0)
    return dict(particles=particles, references=references)


step_size = 0.5


def kernel_terms(block, others):
    inner = jnp.dot(block, others.T, precision=lax.Precision.HIGHEST, preferred_element_type=jnp.float32)
    squared = jnp.sum(block * block, axis=1)[:, None] + jnp.sum(others * others, axis=1)[None, :] - 2.0 * inner
    weights = jnp.exp(-0.5 * squared)
    pulled = jnp.dot(weights, others, precision=lax.Precision.HIGHEST, preferred_element_type=jnp.float32)
    return pulled, jnp.sum(weights, axis=1)


def reference(particles, references):
    count_p = particles.shape[0]
    count_r = references.shape[0]
    width = particles.shape[1]
    blocks = count_p // (ROWS_DEV * N_REF)
    current = particles
    for step in range(STEPS):
        def one_block(block):
            pull_p, sum_p = kernel_terms(block, current)
            pull_r, sum_r = kernel_terms(block, references)
            return (pull_p - sum_p[:, None] * block) / count_p - (pull_r - sum_r[:, None] * block) / count_r
        gradient = lax.map(one_block, current.reshape(blocks, count_p // blocks, width)).reshape(count_p, width)
        current = current - step_size * gradient
    return current, (current - particles) / step_size
```

```python
import functools

import jax
import jax.numpy as jnp
from jax import lax
from jax.experimental import pallas as pl
from jax.experimental.pallas import tpu as pltpu
from jax.sharding import PartitionSpec as P

STEPS = 2


step_size = 0.5
LOG2E = 1.4426950408889634
TILE = 1024
OVER_WIDTH = (((1,), (1,)), ((), ()))


def split(values):
    high = values.astype(jnp.bfloat16)
    return high, (values - high.astype(jnp.float32)).astype(jnp.bfloat16)


def left_operand(block):
    high, low = split(block * LOG2E)
    return jnp.concatenate(
        [jnp.concatenate([high, high], axis=1), jnp.concatenate([low, low], axis=1)], axis=0
    )


def kernel_terms(left, left_square, others):
    rows = left.shape[0] // 2
    width = others.shape[1]
    high, low = split(others)
    right = jnp.concatenate([high, low], axis=1)
    square = jnp.transpose(jnp.sum(others * others, axis=1, keepdims=True)) * (-0.5 * LOG2E)
    both = lax.dot_general(left, right, OVER_WIDTH, preferred_element_type=jnp.float32)
    weights = jnp.exp2(both[:rows] + both[rows:] + (left_square + square))
    weights_high, weights_low = split(weights)
    pulled = jnp.dot(
        jnp.concatenate([weights_high, weights_low], axis=0), right, preferred_element_type=jnp.float32
    )
    pulled = pulled[:rows] + pulled[rows:]
    return pulled[:, :width] + pulled[:, width:], jnp.sum(weights, axis=1, keepdims=True)


def all_terms(block, others_ref):
    left = left_operand(block)
    left_square = jnp.sum(block * block, axis=1, keepdims=True) * (-0.5 * LOG2E)
    count = others_ref.shape[0]
    tile = min(TILE, count)
    pulled = jnp.zeros(block.shape, jnp.float32)
    summed = jnp.zeros((block.shape[0], 1), jnp.float32)
    for start in range(0, count, tile):
        more = kernel_terms(left, left_square, others_ref[pl.ds(start, tile), :])
        pulled, summed = pulled + more[0], summed + more[1]
    return pulled - summed * block


def references_kernel(count_r, block_ref, others_ref, out_ref):
    out_ref[...] = all_terms(block_ref[...], others_ref) * (-1.0 / count_r)


def partners_kernel(count_p, block_ref, first_ref, *refs):
    other_refs, out_ref = refs[:-1], refs[-1]
    total = first_ref[...]
    for other in other_refs:
        total += all_terms(block_ref[...], other) * (1.0 / count_p)
    out_ref[...] = total


def on_vmem(body, rows, *args):
    return pl.pallas_call(
        body,
        out_shape=jax.ShapeDtypeStruct((rows, args[0].shape[1]), jnp.float32),
        in_specs=[pl.BlockSpec(memory_space=pltpu.VMEM)] * len(args),
        out_specs=pl.BlockSpec(memory_space=pltpu.VMEM),
        compiler_params=pltpu.CompilerParams(vmem_limit_bytes=40 << 20),
        cost_estimate=pl.CostEstimate(
            flops=8 * rows * args[1].shape[0] * args[0].shape[1],
            bytes_accessed=4 * sum(a.size for a in args),
            transcendentals=rows * args[1].shape[0],
        ),
    )(*args)


def exchange(values, axis, offset):
    size = lax.axis_size(axis)
    return lax.ppermute(values, axis, [(i, i ^ offset) for i in range(size)])


def offsets_of(n_dom, n_ref):
    share = n_dom // n_ref
    order = [0, 2, 1, 3] if n_ref == 4 else list(range(n_ref))
    return [[order[r] * share + i for i in range(share)] for r in range(n_ref)]


def partner_blocks(block, n_dom, n_ref):
    offsets = offsets_of(n_dom, n_ref)
    blocks = []
    for i in range(n_dom // n_ref):
        pairs = [
            (d * n_ref + r, (d ^ offsets[r][i]) * n_ref + r)
            for d in range(n_dom)
            for r in range(n_ref)
            if offsets[r][i]
        ]
        came = lax.ppermute(block, ("dom", "ref"), pairs)
        own = [r for r in range(n_ref) if not offsets[r][i]]
        if own:
            came = jnp.where(lax.axis_index("ref") == own[0], block, came)
        blocks.append(came)
    return blocks


def on_device(particles, references):
    n_ref = lax.axis_size("ref")
    n_dom = lax.axis_size("dom")
    block_rows = particles.shape[0]
    rows = block_rows // n_ref
    count_p = block_rows * n_dom
    count_r = references.shape[0] * n_ref
    place = lax.axis_index("ref")
    start_rows = lax.dynamic_slice_in_dim(particles, place * rows, rows, 0)
    block = particles
    for step in range(STEPS):
        partners = partner_blocks(block, n_dom, n_ref)
        partial_value = on_vmem(
            functools.partial(references_kernel, count_r), block_rows, block, references
        )
        partial_value = on_vmem(
            functools.partial(partners_kernel, count_p), block_rows, block, partial_value, *partners
        )
        if step + 1 < STEPS:
            offset = 1
            while offset < n_ref:
                partial_value = partial_value + exchange(partial_value, "ref", offset)
                offset *= 2
            block = block - step_size * partial_value
        else:
            total = lax.dynamic_slice_in_dim(partial_value, place * rows, rows, 0)
            for offset in range(1, n_ref):
                chunk = lax.dynamic_slice_in_dim(partial_value, (place ^ offset) * rows, rows, 0)
                total = total + exchange(chunk, "ref", offset)
            own_rows = lax.dynamic_slice_in_dim(block, place * rows, rows, 0)
            own_rows = own_rows - step_size * total
    return (own_rows, (own_rows - start_rows) / step_size)


def solution(mesh):
    placed = (P("dom", None), P("ref", None))
    return jax.shard_map(
        on_device,
        mesh=mesh,
        in_specs=placed,
        out_specs=(P(("dom", "ref"), None), P(("dom", "ref"), None)),
        check_vma=False,
    )
```

```python
import functools

import jax
import jax.numpy as jnp
from jax import lax
from jax.experimental import pallas as pl
from jax.experimental.pallas import tpu as pltpu
from jax.sharding import PartitionSpec as P

STEPS = 2


step_size = 0.5
LOG2E = 1.4426950408889634
TILE = 1024
OVER_WIDTH = (((1,), (1,)), ((), ()))


def split(values):
    high = values.astype(jnp.bfloat16)
    return high, (values - high.astype(jnp.float32)).astype(jnp.bfloat16)


def left_operand(block):
    high, low = split(block * LOG2E)
    return jnp.concatenate(
        [jnp.concatenate([high, high], axis=1), jnp.concatenate([low, low], axis=1)], axis=0
    )


def kernel_terms(left, left_square, others):
    rows = left.shape[0] // 2
    width = others.shape[1]
    high, low = split(others)
    right = jnp.concatenate([high, low], axis=1)
    square = jnp.transpose(jnp.sum(others * others, axis=1, keepdims=True)) * (-0.5 * LOG2E)
    both = lax.dot_general(left, right, OVER_WIDTH, preferred_element_type=jnp.float32)
    weights = jnp.exp2(both[:rows] + both[rows:] + (left_square + square))
    weights_high, weights_low = split(weights)
    pulled = jnp.dot(
        jnp.concatenate([weights_high, weights_low], axis=0), right, preferred_element_type=jnp.float32
    )
    pulled = pulled[:rows] + pulled[rows:]
    return pulled[:, :width] + pulled[:, width:], jnp.sum(weights, axis=1, keepdims=True)


def tiles_of(others):
    count = sum(other.shape[0] for other in others)
    if count <= TILE:
        return [jnp.concatenate([other[...] for other in others], axis=0)]
    return [
        other[pl.ds(start, min(TILE, other.shape[0])), :]
        for other in others
        for start in range(0, other.shape[0], TILE)
    ]


def all_terms(block, others):
    left = left_operand(block)
    left_square = jnp.sum(block * block, axis=1, keepdims=True) * (-0.5 * LOG2E)
    pulled = jnp.zeros(block.shape, jnp.float32)
    summed = jnp.zeros((block.shape[0], 1), jnp.float32)
    for tile in tiles_of(others):
        more = kernel_terms(left, left_square, tile)
        pulled, summed = pulled + more[0], summed + more[1]
    return pulled - summed * block


def references_kernel(count_r, block_ref, others_ref, out_ref, *own_refs):
    out_ref[...] = all_terms(block_ref[...], [others_ref]) * (-1.0 / count_r)
    for own_ref in own_refs:
        rows = own_ref.shape[0]
        own_ref[...] = block_ref[pl.ds(pl.multiple_of(lax.axis_index("ref") * rows, rows), rows), :]


def partners_kernel(count_p, block_ref, first_ref, *refs):
    other_refs, out_ref = refs[:-1], refs[-1]
    out_ref[...] = first_ref[...] + all_terms(block_ref[...], other_refs) * (1.0 / count_p)


def on_vmem(body, rows, *args):
    return pl.pallas_call(
        body,
        out_shape=[jax.ShapeDtypeStruct((r, args[0].shape[1]), jnp.float32) for r in rows],
        in_specs=[pl.BlockSpec(memory_space=pltpu.VMEM)] * len(args),
        out_specs=[pl.BlockSpec(memory_space=pltpu.VMEM)] * len(rows),
        compiler_params=pltpu.CompilerParams(vmem_limit_bytes=40 << 20),
        cost_estimate=pl.CostEstimate(
            flops=8 * rows[0] * args[1].shape[0] * args[0].shape[1],
            bytes_accessed=4 * sum(a.size for a in args),
            transcendentals=rows[0] * args[1].shape[0],
        ),
    )(*args)


def exchange(values, axis, offset):
    size = lax.axis_size(axis)
    return lax.ppermute(values, axis, [(i, i ^ offset) for i in range(size)])


def offsets_of(n_dom, n_ref):
    share = n_dom // n_ref
    return [
        [i * n_ref + (r if i % 2 == 0 else n_ref - 1 - r) for i in reversed(range(share))]
        for r in range(n_ref)
    ]


def partner_blocks(block, n_dom, n_ref):
    offsets = offsets_of(n_dom, n_ref)
    blocks = []
    for i in range(n_dom // n_ref):
        pairs = [
            (d * n_ref + r, (d ^ offsets[r][i]) * n_ref + r)
            for d in range(n_dom)
            for r in range(n_ref)
        ]
        blocks.append(lax.ppermute(block, ("dom", "ref"), pairs))
    return blocks


def on_device(particles, references):
    n_ref = lax.axis_size("ref")
    n_dom = lax.axis_size("dom")
    block_rows = particles.shape[0]
    rows = block_rows // n_ref
    count_p = block_rows * n_dom
    count_r = references.shape[0] * n_ref
    place = lax.axis_index("ref")
    block = particles
    for step in range(STEPS):
        partners = partner_blocks(block, n_dom, n_ref)
        partial_value, *own = on_vmem(
            functools.partial(references_kernel, count_r),
            [block_rows, rows],
            block,
            references,
        )
        if step == 0:
            start_rows = own[0]
        (partial_value,) = on_vmem(
            functools.partial(partners_kernel, count_p), [block_rows], block, partial_value, *partners
        )
        if step + 1 < STEPS:
            offset = 1
            while offset < n_ref:
                partial_value = partial_value + exchange(partial_value, "ref", offset)
                offset *= 2
            block = block - step_size * partial_value
        else:
            total = lax.dynamic_slice_in_dim(partial_value, place * rows, rows, 0)
            for offset in range(1, n_ref):
                chunk = lax.dynamic_slice_in_dim(partial_value, (place ^ offset) * rows, rows, 0)
                total = total + exchange(chunk, "ref", offset)
            own_rows = own[0] - step_size * total
    return (own_rows, (own_rows - start_rows) / step_size)


def solution(mesh):
    placed = (P("dom", None), P("ref", None))
    return jax.shard_map(
        on_device,
        mesh=mesh,
        in_specs=placed,
        out_specs=(P(("dom", "ref"), None), P(("dom", "ref"), None)),
        check_vma=False,
    )
```

```python
import functools

import jax
import jax.numpy as jnp
from jax import lax
from jax.experimental import pallas as pl
from jax.experimental.pallas import tpu as pltpu
from jax.sharding import PartitionSpec as P

STEPS = 2


step_size = 0.5
LOG2E = 1.4426950408889634
TILE = 1024
VMEM_BYTES = 48 << 20
OVER_WIDTH = (((1,), (1,)), ((), ()))
IN_VMEM = pl.BlockSpec(memory_space=pltpu.VMEM)


def split(values):
    high = values.astype(jnp.bfloat16)
    return high, (values - high.astype(jnp.float32)).astype(jnp.bfloat16)


def half_square(values):
    return jnp.sum(values * values, axis=1, keepdims=True) * (-0.5 * LOG2E)


def left_operand(block):
    high, low = split(block * LOG2E)
    return jnp.concatenate(
        [jnp.concatenate([high, high], axis=1), jnp.concatenate([low, low], axis=1)], axis=0
    )


def prepare(others):
    return jnp.concatenate(split(others), axis=1), jnp.transpose(half_square(others))


def kernel_terms(left, left_square, right, square):
    rows = left.shape[0] // 2
    width = right.shape[1] // 2
    both = lax.dot_general(left, right, OVER_WIDTH, preferred_element_type=jnp.float32)
    weights = jnp.exp2(both[:rows] + both[rows:] + (left_square + square))
    pulled = jnp.dot(
        jnp.concatenate(split(weights), axis=0), right, preferred_element_type=jnp.float32
    )
    pulled = pulled[:rows] + pulled[rows:]
    return pulled[:, :width] + pulled[:, width:], jnp.sum(weights, axis=1, keepdims=True)


def all_terms(block, pieces):
    left = left_operand(block)
    left_square = half_square(block)
    pulled = jnp.zeros(block.shape, jnp.float32)
    summed = jnp.zeros((block.shape[0], 1), jnp.float32)
    for right, square in pieces:
        count = right.shape[0]
        for start in range(0, count, TILE):
            tile = slice(start, min(start + TILE, count))
            more = kernel_terms(left, left_square, right[tile, :], square[:, tile])
            pulled, summed = pulled + more[0], summed + more[1]
    return pulled - summed * block


def joined(refs):
    return jnp.concatenate([ref[...] for ref in refs], axis=0) if len(refs) > 1 else refs[0][...]


def own_slice(ref, rows):
    return ref[pl.ds(pl.multiple_of(lax.axis_index("ref") * rows, rows), rows), :]


def f32(*shape):
    return jax.ShapeDtypeStruct(shape, jnp.float32)


def exchange(values, axis, offset):
    size = lax.axis_size(axis)
    return lax.ppermute(values, axis, [(i, i ^ offset) for i in range(size)])


def after(values, *earlier):
    return lax.optimization_barrier((values,) + earlier)[0]


def references_kernel(count_r, block_ref, others_ref, out_ref, own_ref):
    block = block_ref[...]
    out_ref[...] = all_terms(block, [prepare(others_ref[...])]) * (-1.0 / count_r)
    own_ref[...] = own_slice(block_ref, own_ref.shape[0])


def partners_kernel(count_p, block_ref, first_ref, *refs):
    other_refs, out_ref = refs[:-1], refs[-1]
    others = prepare(joined(other_refs))
    out_ref[...] = first_ref[...] + all_terms(block_ref[...], [others]) * (1.0 / count_p)


def on_vmem(body, rows, *args):
    return pl.pallas_call(
        body,
        out_shape=[f32(r, args[0].shape[1]) for r in rows],
        in_specs=[IN_VMEM] * len(args),
        out_specs=[IN_VMEM] * len(rows),
        compiler_params=pltpu.CompilerParams(vmem_limit_bytes=VMEM_BYTES),
        cost_estimate=pl.CostEstimate(
            flops=8 * rows[0] * args[1].shape[0] * args[0].shape[1],
            bytes_accessed=4 * sum(a.size for a in args),
            transcendentals=rows[0] * args[1].shape[0],
        ),
    )(*args)


def offsets_of(n_dom, n_ref):
    share = n_dom // n_ref
    return [
        [i * n_ref + (r if i % 2 == 0 else n_ref - 1 - r) for i in reversed(range(share))]
        for r in range(n_ref)
    ]


def partner_blocks(block, n_dom, n_ref):
    offsets = offsets_of(n_dom, n_ref)
    blocks = []
    for i in range(n_dom // n_ref):
        pairs = [
            (d * n_ref + r, (d ^ offsets[r][i]) * n_ref + r)
            for d in range(n_dom)
            for r in range(n_ref)
        ]
        blocks.append(lax.ppermute(block, ("dom", "ref"), pairs))
    return blocks


def exchange_plan(particles, references):
    n_ref = lax.axis_size("ref")
    n_dom = lax.axis_size("dom")
    block_rows = particles.shape[0]
    rows = block_rows // n_ref
    count_p = block_rows * n_dom
    count_r = references.shape[0] * n_ref
    place = lax.axis_index("ref")
    block = particles
    for step in range(STEPS):
        partners = partner_blocks(block, n_dom, n_ref)
        partial_value, own = on_vmem(
            functools.partial(references_kernel, count_r),
            [block_rows, rows],
            block,
            references,
        )
        if step == 0:
            start_rows = own
        (partial_value,) = on_vmem(
            functools.partial(partners_kernel, count_p), [block_rows], block, partial_value, *partners
        )
        if step + 1 < STEPS:
            offset = 1
            while offset < n_ref:
                partial_value = partial_value + exchange(partial_value, "ref", offset)
                offset *= 2
            block = block - step_size * partial_value
        else:
            total = lax.dynamic_slice_in_dim(partial_value, place * rows, rows, 0)
            for offset in range(1, n_ref):
                chunk = lax.dynamic_slice_in_dim(partial_value, (place ^ offset) * rows, rows, 0)
                total = total + exchange(chunk, "ref", offset)
            own_rows = own - step_size * total
    return (own_rows, (own_rows - start_rows) / step_size)


def pull_kernel(scales, counts, has_first, moves, last, own_rows, *refs):
    refs = list(refs)

    def take(count):
        return [refs.pop(0) for _ in range(count)]

    (rows_ref,) = take(1)
    groups = [(take(raw), [tuple(take(2)) for _ in range(pairs)]) for raw, pairs in counts]
    first_refs = take(has_first)
    start_refs = take(last)
    copied_refs = take(own_rows > 0)
    (out_ref,) = take(1)
    rows = rows_ref[...]
    total = first_refs[0][...] if has_first else jnp.zeros(rows.shape, jnp.float32)
    if last:
        (drift_ref,) = take(1)
    if copied_refs:
        copy_ref, own_ref = take(2)
        copy_ref[...] = copied_refs[0][...]
        own_ref[...] = own_slice(copied_refs[0], own_rows)
    for scale, (raw, pairs) in zip(scales, groups):
        pieces = []
        if raw:
            pieces.append(prepare(joined(raw)))
            for ref, value in zip(take(2), pieces[0]):
                ref[...] = value
        pieces += [(right[...], square[...]) for right, square in pairs]
        total += all_terms(rows, pieces) * scale
    if moves:
        total = rows - step_size * total
    out_ref[...] = total
    if last:
        drift_ref[...] = (total - start_refs[0][...]) / step_size


def pull(rows, groups, first=None, moves=False, start=None, copied=None, own_rows=0):
    count, width = rows.shape
    args, outs = [rows], [f32(count, width)]
    if start is not None:
        outs.append(f32(count, width))
    if copied is not None:
        outs += [f32(*copied.shape), f32(own_rows, width)]
    results = len(outs)
    for _, raw, pairs in groups:
        args += list(raw) + [value for pair in pairs for value in pair]
        if raw:
            size = sum(r.shape[0] for r in raw)
            outs += [jax.ShapeDtypeStruct((size, 2 * width), jnp.bfloat16), f32(1, size)]
    args += [value for value in (first, start, copied) if value is not None]
    body = functools.partial(
        pull_kernel,
        [scale for scale, _, _ in groups],
        [(len(raw), len(pairs)) for _, raw, pairs in groups],
        int(first is not None),
        moves,
        int(start is not None),
        own_rows,
    )
    got = pl.pallas_call(
        body,
        out_shape=outs,
        in_specs=[IN_VMEM] * len(args),
        out_specs=[IN_VMEM] * len(outs),
        compiler_params=pltpu.CompilerParams(vmem_limit_bytes=VMEM_BYTES),
        cost_estimate=pl.CostEstimate(flops=1, bytes_accessed=1, transcendentals=0),
    )(*args)
    prepared = [tuple(got[i : i + 2]) for i in range(results, len(got), 2)]
    return list(got[:results]) + prepared


def by_core(values, offsets, n_dom, n_ref):
    pairs = [
        (d * n_ref + r, (d ^ offsets[r % 2]) * n_ref + r) for d in range(n_dom) for r in range(n_ref)
    ]
    return lax.ppermute(values, ("dom", "ref"), pairs)


def gather_plan(particles, references):
    n_ref = lax.axis_size("ref")
    n_dom = lax.axis_size("dom")
    block_rows = particles.shape[0]
    rows = block_rows // n_ref
    for_p = 1.0 / (block_rows * n_dom)
    for_r = -1.0 / (references.shape[0] * n_ref)
    place = lax.axis_index("ref")
    core = place % 2

    across = exchange(references, "ref", 2)
    near = by_core(particles, (2, 1), n_dom, n_ref)
    far = by_core(particles, (6, 7), n_dom, n_ref)
    middle = by_core(particles, (4, 5), n_dom, n_ref)
    mate = exchange(references, "ref", 1)

    near_sum, mate_pair = pull(near, [(for_r, [mate], [])])
    near_sum, own_pair = pull(near, [(for_r, [references], [])], near_sum)
    at_hand = [mate_pair, own_pair]
    relay_pairs = [
        (d * n_ref + r, (d ^ 1) * n_ref + r + 1) for d in range(n_dom) for r in range(0, n_ref, 2)
    ]
    relayed = lax.ppermute(after(near, near_sum), ("dom", "ref"), relay_pairs)
    far_sum, block, start_rows = pull(
        after(far, near_sum), [(for_r, [], at_hand)], copied=particles, own_rows=rows
    )
    middle_sum = pull(after(middle, far_sum), [(for_r, [], at_hand)])[0]
    fourth = jnp.where(core == 0, block, after(relayed, middle_sum))
    fourth_sum = pull(fourth, [(for_r, [], at_hand)])[0]

    held = jnp.concatenate([near, far, middle, fourth])
    held_sum = jnp.concatenate([near_sum, far_sum, middle_sum, fourth_sum])
    held_by_mate = exchange(held, "ref", 1)
    across = after(across, fourth_sum)
    across_mate = exchange(across, "ref", 1)
    held_sum, across_pair = pull(held, [(for_r, [across], [])], held_sum)
    held_sum = pull(held, [(for_p, [held, held_by_mate], [])], held_sum)[0]
    moved, across_mate_pair = pull(held, [(for_r, [across_mate], [])], held_sum, moves=True)

    moved_by_mate = exchange(moved, "ref", 1)
    own_block = jnp.where(core == 0, moved[3 * block_rows :], moved_by_mate[3 * block_rows :])
    own_rows = lax.dynamic_slice_in_dim(own_block, place * rows, rows, 0)
    groups = [
        (for_p, [moved, moved_by_mate], []),
        (for_r, [], at_hand + [across_pair, across_mate_pair]),
    ]
    return tuple(pull(own_rows, groups, moves=True, start=start_rows)[:2])


def on_device(particles, references):
    if (lax.axis_size("dom"), lax.axis_size("ref")) == (8, 4) and STEPS == 2:
        return gather_plan(particles, references)
    return exchange_plan(particles, references)


def solution(mesh):
    placed = (P("dom", None), P("ref", None))
    return jax.shard_map(
        on_device,
        mesh=mesh,
        in_specs=placed,
        out_specs=(P(("dom", "ref"), None), P(("dom", "ref"), None)),
        check_vma=False,
    )
```

```python
import functools

import jax
import jax.numpy as jnp
from jax import lax
from jax.experimental import pallas as pl
from jax.experimental.pallas import tpu as pltpu
from jax.sharding import PartitionSpec as P

STEPS = 2


step_size = 0.5
LOG2E = 1.4426950408889634
TILE = 1024
VMEM_BYTES = 48 << 20
OVER_WIDTH = (((1,), (1,)), ((), ()))
IN_VMEM = pl.BlockSpec(memory_space=pltpu.VMEM)


def split(values):
    high = values.astype(jnp.bfloat16)
    return high, (values - high.astype(jnp.float32)).astype(jnp.bfloat16)


def half_square(values):
    return jnp.sum(values * values, axis=1, keepdims=True) * (-0.5 * LOG2E)


def left_operand(block):
    high, low = split(block * LOG2E)
    return jnp.concatenate(
        [jnp.concatenate([high, high], axis=1), jnp.concatenate([low, low], axis=1)], axis=0
    )


def prepare(others):
    return jnp.concatenate(split(others), axis=1), jnp.transpose(half_square(others))


def kernel_terms(left, left_square, right, square):
    rows = left.shape[0] // 2
    width = right.shape[1] // 2
    both = lax.dot_general(left, right, OVER_WIDTH, preferred_element_type=jnp.float32)
    weights = jnp.exp2(both[:rows] + both[rows:] + (left_square + square))
    pulled = jnp.dot(
        jnp.concatenate(split(weights), axis=0), right, preferred_element_type=jnp.float32
    )
    pulled = pulled[:rows] + pulled[rows:]
    return pulled[:, :width] + pulled[:, width:], jnp.sum(weights, axis=1, keepdims=True)


def all_terms(block, pieces):
    left = left_operand(block)
    left_square = half_square(block)
    pulled = jnp.zeros(block.shape, jnp.float32)
    summed = jnp.zeros((block.shape[0], 1), jnp.float32)
    for right, square in pieces:
        count = right.shape[0]
        for start in range(0, count, TILE):
            tile = slice(start, min(start + TILE, count))
            more = kernel_terms(left, left_square, right[tile, :], square[:, tile])
            pulled, summed = pulled + more[0], summed + more[1]
    return pulled - summed * block


def joined(refs):
    return jnp.concatenate([ref[...] for ref in refs], axis=0) if len(refs) > 1 else refs[0][...]


def own_slice(ref, rows):
    return ref[pl.ds(pl.multiple_of(lax.axis_index("ref") * rows, rows), rows), :]


def f32(*shape):
    return jax.ShapeDtypeStruct(shape, jnp.float32)


def exchange(values, axis, offset):
    size = lax.axis_size(axis)
    return lax.ppermute(values, axis, [(i, i ^ offset) for i in range(size)])


def after(values, *earlier):
    return lax.optimization_barrier((values,) + earlier)[0]


def references_kernel(count_r, block_ref, others_ref, out_ref, own_ref):
    block = block_ref[...]
    out_ref[...] = all_terms(block, [prepare(others_ref[...])]) * (-1.0 / count_r)
    own_ref[...] = own_slice(block_ref, own_ref.shape[0])


def partners_kernel(count_p, block_ref, first_ref, *refs):
    other_refs, out_ref = refs[:-1], refs[-1]
    others = prepare(joined(other_refs))
    out_ref[...] = first_ref[...] + all_terms(block_ref[...], [others]) * (1.0 / count_p)


def on_vmem(body, rows, *args):
    return pl.pallas_call(
        body,
        out_shape=[f32(r, args[0].shape[1]) for r in rows],
        in_specs=[IN_VMEM] * len(args),
        out_specs=[IN_VMEM] * len(rows),
        compiler_params=pltpu.CompilerParams(vmem_limit_bytes=VMEM_BYTES),
        cost_estimate=pl.CostEstimate(
            flops=8 * rows[0] * args[1].shape[0] * args[0].shape[1],
            bytes_accessed=4 * sum(a.size for a in args),
            transcendentals=rows[0] * args[1].shape[0],
        ),
    )(*args)


def offsets_of(n_dom, n_ref):
    share = n_dom // n_ref
    return [
        [i * n_ref + (r if i % 2 == 0 else n_ref - 1 - r) for i in reversed(range(share))]
        for r in range(n_ref)
    ]


def partner_blocks(block, n_dom, n_ref):
    offsets = offsets_of(n_dom, n_ref)
    blocks = []
    for i in range(n_dom // n_ref):
        pairs = [
            (d * n_ref + r, (d ^ offsets[r][i]) * n_ref + r)
            for d in range(n_dom)
            for r in range(n_ref)
        ]
        blocks.append(lax.ppermute(block, ("dom", "ref"), pairs))
    return blocks


def exchange_plan(particles, references):
    n_ref = lax.axis_size("ref")
    n_dom = lax.axis_size("dom")
    block_rows = particles.shape[0]
    rows = block_rows // n_ref
    count_p = block_rows * n_dom
    count_r = references.shape[0] * n_ref
    place = lax.axis_index("ref")
    block = particles
    for step in range(STEPS):
        partners = partner_blocks(block, n_dom, n_ref)
        partial_value, own = on_vmem(
            functools.partial(references_kernel, count_r),
            [block_rows, rows],
            block,
            references,
        )
        if step == 0:
            start_rows = own
        (partial_value,) = on_vmem(
            functools.partial(partners_kernel, count_p), [block_rows], block, partial_value, *partners
        )
        if step + 1 < STEPS:
            offset = 1
            while offset < n_ref:
                partial_value = partial_value + exchange(partial_value, "ref", offset)
                offset *= 2
            block = block - step_size * partial_value
        else:
            total = lax.dynamic_slice_in_dim(partial_value, place * rows, rows, 0)
            for offset in range(1, n_ref):
                chunk = lax.dynamic_slice_in_dim(partial_value, (place ^ offset) * rows, rows, 0)
                total = total + exchange(chunk, "ref", offset)
            own_rows = own - step_size * total
    return (own_rows, (own_rows - start_rows) / step_size)


def pull_kernel(scales, counts, has_first, moves, last, cut, prepares, *refs):
    refs = list(refs)

    def take(count):
        return [refs.pop(0) for _ in range(count)]

    (rows_ref,) = take(1)
    groups = [(take(raw), [tuple(take(2)) for _ in range(pairs)]) for raw, pairs in counts]
    first_refs = take(has_first)
    start_refs = take(last)
    whole_refs = take(cut)
    prepare_refs = take(prepares)
    (out_ref,) = take(1)
    drift_refs = take(last)
    if cut:
        cut_block(whole_refs[0], *take(3))
    rows = rows_ref[...]
    total = first_refs[0][...] if has_first else jnp.zeros(rows.shape, jnp.float32)
    for scale, (raw, pairs) in zip(scales, groups):
        pieces = []
        if raw:
            pieces.append(prepare(joined(raw)))
            for ref, value in zip(take(2), pieces[0]):
                ref[...] = value
        pieces += [(right[...], square[...]) for right, square in pairs]
        total += all_terms(rows, pieces) * scale
    if prepares:
        for ref, value in zip(take(2), prepare(prepare_refs[0][...])):
            ref[...] = value
    if moves:
        total = rows - step_size * total
    out_ref[...] = total
    if last:
        drift_refs[0][...] = (total - start_refs[0][...]) / step_size


def cut_block(block_ref, mine_ref, half_ref, start_ref):
    place = lax.axis_index("ref")
    core = lax.rem(place, 2)
    rows, half = start_ref.shape[0], half_ref.shape[0]

    def part(start, count):
        return block_ref[pl.ds(pl.multiple_of(start, rows), count), :]

    for i in range(mine_ref.shape[0] // rows):
        mine_ref[pl.ds(i * rows, rows), :] = part((2 * i + core) * rows, rows)
    half_ref[...] = part(core * half, half)
    start_ref[...] = part(place * rows, rows)


def pull(rows, groups, first=None, moves=False, start=None, cut=None, prepares=None):
    count, width = rows.shape
    args, outs = [rows], [f32(count, width)]
    if start is not None:
        outs.append(f32(count, width))
    if cut is not None:
        half = cut.shape[0] // 2
        outs += [f32(half, width), f32(half, width), f32(cut.shape[0] // lax.axis_size("ref"), width)]
    results = len(outs)
    for _, raw, pairs in groups:
        args += list(raw) + [value for pair in pairs for value in pair]
        if raw:
            size = sum(r.shape[0] for r in raw)
            outs += [jax.ShapeDtypeStruct((size, 2 * width), jnp.bfloat16), f32(1, size)]
    if prepares is not None:
        size = prepares.shape[0]
        outs += [jax.ShapeDtypeStruct((size, 2 * width), jnp.bfloat16), f32(1, size)]
    args += [value for value in (first, start, cut, prepares) if value is not None]
    body = functools.partial(
        pull_kernel,
        [scale for scale, _, _ in groups],
        [(len(raw), len(pairs)) for _, raw, pairs in groups],
        int(first is not None),
        moves,
        int(start is not None),
        int(cut is not None),
        int(prepares is not None),
    )
    got = pl.pallas_call(
        body,
        out_shape=outs,
        in_specs=[IN_VMEM] * len(args),
        out_specs=[IN_VMEM] * len(outs),
        compiler_params=pltpu.CompilerParams(vmem_limit_bytes=VMEM_BYTES),
        cost_estimate=pl.CostEstimate(flops=1, bytes_accessed=1, transcendentals=0),
    )(*args)
    prepared = [tuple(got[i : i + 2]) for i in range(results, len(got), 2)]
    return list(got[:results]) + prepared


def by_core(values, offsets, n_dom, n_ref):
    pairs = [
        (d * n_ref + r, (d ^ offsets[r % 2]) * n_ref + r) for d in range(n_dom) for r in range(n_ref)
    ]
    return lax.ppermute(values, ("dom", "ref"), pairs)


def gather_plan(particles, references):
    n_ref = lax.axis_size("ref")
    n_dom = lax.axis_size("dom")
    block_rows = particles.shape[0]
    rows = block_rows // n_ref
    for_p = 1.0 / (block_rows * n_dom)
    for_r = -1.0 / (references.shape[0] * n_ref)
    place = lax.axis_index("ref")

    across = exchange(references, "ref", 2)
    near = by_core(particles, (2, 3), n_dom, n_ref)
    far = by_core(particles, (6, 7), n_dom, n_ref)
    middle = by_core(particles, (4, 5), n_dom, n_ref)
    mate = exchange(references, "ref", 1)

    near_sum, mate_pair = pull(near, [(for_r, [mate], [])])
    near_sum, mine, half, start_rows, own_pair = pull(
        near, [(for_r, [references], [])], near_sum, cut=particles
    )
    at_hand = [mate_pair, own_pair]
    beside = exchange(half, "dom", 1)
    far_sum = pull(after(far, near_sum), [(for_r, [], at_hand)])[0]
    fourth = jnp.concatenate([mine, after(beside, far_sum)])
    fourth_sum = pull(fourth, [(for_r, [], at_hand)])[0]
    middle = after(middle, fourth_sum)
    middle_sum = pull(middle, [(for_r, [], at_hand)])[0]

    held = jnp.concatenate([near, far, fourth, middle])
    held_sum = jnp.concatenate([near_sum, far_sum, fourth_sum, middle_sum])
    held_by_mate = exchange(held, "ref", 1)
    across = after(across, middle_sum)
    across_mate = exchange(across, "ref", 1)
    held_sum, across_pair = pull(held, [(for_r, [across], [])], held_sum)
    groups = [(for_p, [held, held_by_mate], []), (for_r, [across_mate], [])]
    moved, _, across_mate_pair = pull(held, groups, held_sum, moves=True)

    moved_by_mate = exchange(moved, "ref", 1)
    own_rows = lax.dynamic_slice_in_dim(moved, 2 * block_rows + (place // 2) * rows, rows, 0)
    groups = [(for_r, [], at_hand + [across_pair, across_mate_pair])]
    own_sum, moved_pair = pull(own_rows, groups, prepares=moved)
    groups = [(for_p, [moved_by_mate], [moved_pair])]
    return tuple(pull(own_rows, groups, own_sum, moves=True, start=start_rows)[:2])


def on_device(particles, references):
    if (lax.axis_size("dom"), lax.axis_size("ref")) == (8, 4) and STEPS == 2:
        return gather_plan(particles, references)
    return exchange_plan(particles, references)


def solution(mesh):
    placed = (P("dom", None), P("ref", None))
    return jax.shard_map(
        on_device,
        mesh=mesh,
        in_specs=placed,
        out_specs=(P(("dom", "ref"), None), P(("dom", "ref"), None)),
        check_vma=False,
    )
```

```python
import functools

import jax
import jax.numpy as jnp
from jax import lax
from jax.experimental import pallas as pl
from jax.experimental.pallas import tpu as pltpu
from jax.sharding import PartitionSpec as P

STEPS = 2


step_size = 0.5
LOG2E = 1.4426950408889634
TILE = 1024
VMEM_BYTES = 48 << 20
OVER_WIDTH = (((1,), (1,)), ((), ()))
IN_VMEM = pl.BlockSpec(memory_space=pltpu.VMEM)


def split(values):
    high = values.astype(jnp.bfloat16)
    return high, (values - high.astype(jnp.float32)).astype(jnp.bfloat16)


def half_square(values):
    return jnp.sum(values * values, axis=1, keepdims=True) * (-0.5 * LOG2E)


def left_operand(block):
    high, low = split(block * LOG2E)
    return jnp.concatenate(
        [jnp.concatenate([high, high], axis=1), jnp.concatenate([low, low], axis=1)], axis=0
    )


def prepare(others):
    return jnp.concatenate(split(others), axis=1), jnp.transpose(half_square(others))


def kernel_terms(left, left_square, right, square):
    rows = left.shape[0] // 2
    width = right.shape[1] // 2
    both = lax.dot_general(left, right, OVER_WIDTH, preferred_element_type=jnp.float32)
    weights = jnp.exp2(both[:rows] + both[rows:] + (left_square + square))
    pulled = jnp.dot(
        jnp.concatenate(split(weights), axis=0), right, preferred_element_type=jnp.float32
    )
    pulled = pulled[:rows] + pulled[rows:]
    return pulled[:, :width] + pulled[:, width:], jnp.sum(weights, axis=1, keepdims=True)


def all_terms(block, pieces):
    left = left_operand(block)
    left_square = half_square(block)
    pulled = jnp.zeros(block.shape, jnp.float32)
    summed = jnp.zeros((block.shape[0], 1), jnp.float32)
    for right, square in pieces:
        count = right.shape[0]
        for start in range(0, count, TILE):
            tile = slice(start, min(start + TILE, count))
            more = kernel_terms(left, left_square, right[tile, :], square[:, tile])
            pulled, summed = pulled + more[0], summed + more[1]
    return pulled - summed * block


def joined(refs):
    return jnp.concatenate([ref[...] for ref in refs], axis=0) if len(refs) > 1 else refs[0][...]


def own_slice(ref, rows):
    return ref[pl.ds(pl.multiple_of(lax.axis_index("ref") * rows, rows), rows), :]


def f32(*shape):
    return jax.ShapeDtypeStruct(shape, jnp.float32)


def exchange(values, axis, offset):
    size = lax.axis_size(axis)
    return lax.ppermute(values, axis, [(i, i ^ offset) for i in range(size)])


def after(values, *earlier):
    return lax.optimization_barrier((values,) + earlier)[0]


def references_kernel(count_r, block_ref, others_ref, out_ref, own_ref):
    block = block_ref[...]
    out_ref[...] = all_terms(block, [prepare(others_ref[...])]) * (-1.0 / count_r)
    own_ref[...] = own_slice(block_ref, own_ref.shape[0])


def partners_kernel(count_p, block_ref, first_ref, *refs):
    other_refs, out_ref = refs[:-1], refs[-1]
    others = prepare(joined(other_refs))
    out_ref[...] = first_ref[...] + all_terms(block_ref[...], [others]) * (1.0 / count_p)


def on_vmem(body, rows, *args):
    return pl.pallas_call(
        body,
        out_shape=[f32(r, args[0].shape[1]) for r in rows],
        in_specs=[IN_VMEM] * len(args),
        out_specs=[IN_VMEM] * len(rows),
        compiler_params=pltpu.CompilerParams(vmem_limit_bytes=VMEM_BYTES),
        cost_estimate=pl.CostEstimate(
            flops=8 * rows[0] * args[1].shape[0] * args[0].shape[1],
            bytes_accessed=4 * sum(a.size for a in args),
            transcendentals=rows[0] * args[1].shape[0],
        ),
    )(*args)


def offsets_of(n_dom, n_ref):
    share = n_dom // n_ref
    return [
        [i * n_ref + (r if i % 2 == 0 else n_ref - 1 - r) for i in reversed(range(share))]
        for r in range(n_ref)
    ]


def partner_blocks(block, n_dom, n_ref):
    offsets = offsets_of(n_dom, n_ref)
    blocks = []
    for i in range(n_dom // n_ref):
        pairs = [
            (d * n_ref + r, (d ^ offsets[r][i]) * n_ref + r)
            for d in range(n_dom)
            for r in range(n_ref)
        ]
        blocks.append(lax.ppermute(block, ("dom", "ref"), pairs))
    return blocks


def exchange_plan(particles, references):
    n_ref = lax.axis_size("ref")
    n_dom = lax.axis_size("dom")
    block_rows = particles.shape[0]
    rows = block_rows // n_ref
    count_p = block_rows * n_dom
    count_r = references.shape[0] * n_ref
    place = lax.axis_index("ref")
    block = particles
    for step in range(STEPS):
        partners = partner_blocks(block, n_dom, n_ref)
        partial_value, own = on_vmem(
            functools.partial(references_kernel, count_r),
            [block_rows, rows],
            block,
            references,
        )
        if step == 0:
            start_rows = own
        (partial_value,) = on_vmem(
            functools.partial(partners_kernel, count_p), [block_rows], block, partial_value, *partners
        )
        if step + 1 < STEPS:
            offset = 1
            while offset < n_ref:
                partial_value = partial_value + exchange(partial_value, "ref", offset)
                offset *= 2
            block = block - step_size * partial_value
        else:
            total = lax.dynamic_slice_in_dim(partial_value, place * rows, rows, 0)
            for offset in range(1, n_ref):
                chunk = lax.dynamic_slice_in_dim(partial_value, (place ^ offset) * rows, rows, 0)
                total = total + exchange(chunk, "ref", offset)
            own_rows = own - step_size * total
    return (own_rows, (own_rows - start_rows) / step_size)


def pull_kernel(scales, counts, has_first, moves, last, cut, prepares, *refs):
    refs = list(refs)

    def take(count):
        return [refs.pop(0) for _ in range(count)]

    (rows_ref,) = take(1)
    groups = [(take(raw), [tuple(take(2)) for _ in range(pairs)]) for raw, pairs in counts]
    first_refs = take(has_first)
    start_refs = take(last)
    whole_refs = take(cut)
    prepare_refs = take(prepares)
    (out_ref,) = take(1)
    drift_refs = take(last)
    if cut:
        cut_block(whole_refs[0], *take(3))
    rows = rows_ref[...]
    total = first_refs[0][...] if has_first else jnp.zeros(rows.shape, jnp.float32)
    for scale, (raw, pairs) in zip(scales, groups):
        pieces = []
        if raw:
            pieces.append(prepare(joined(raw)))
            for ref, value in zip(take(2), pieces[0]):
                ref[...] = value
        pieces += [(right[...], square[...]) for right, square in pairs]
        total += all_terms(rows, pieces) * scale
    if prepares:
        for ref, value in zip(take(2), prepare(prepare_refs[0][...])):
            ref[...] = value
    if moves:
        total = rows - step_size * total
    out_ref[...] = total
    if last:
        drift_refs[0][...] = (total - start_refs[0][...]) / step_size


def cut_block(block_ref, mine_ref, half_ref, start_ref):
    place = lax.axis_index("ref")
    core = lax.rem(place, 2)
    rows, half = start_ref.shape[0], half_ref.shape[0]

    def part(start, count):
        return block_ref[pl.ds(pl.multiple_of(start, rows), count), :]

    for i in range(mine_ref.shape[0] // rows):
        mine_ref[pl.ds(i * rows, rows), :] = part((2 * i + core) * rows, rows)
    half_ref[...] = part(core * half, half)
    start_ref[...] = part(place * rows, rows)


def pull(rows, groups, first=None, moves=False, start=None, cut=None, prepares=None):
    count, width = rows.shape
    args, outs = [rows], [f32(count, width)]
    if start is not None:
        outs.append(f32(count, width))
    if cut is not None:
        half = cut.shape[0] // 2
        outs += [f32(half, width), f32(half, width), f32(cut.shape[0] // lax.axis_size("ref"), width)]
    results = len(outs)
    for _, raw, pairs in groups:
        args += list(raw) + [value for pair in pairs for value in pair]
        if raw:
            size = sum(r.shape[0] for r in raw)
            outs += [jax.ShapeDtypeStruct((size, 2 * width), jnp.bfloat16), f32(1, size)]
    if prepares is not None:
        size = prepares.shape[0]
        outs += [jax.ShapeDtypeStruct((size, 2 * width), jnp.bfloat16), f32(1, size)]
    args += [value for value in (first, start, cut, prepares) if value is not None]
    body = functools.partial(
        pull_kernel,
        [scale for scale, _, _ in groups],
        [(len(raw), len(pairs)) for _, raw, pairs in groups],
        int(first is not None),
        moves,
        int(start is not None),
        int(cut is not None),
        int(prepares is not None),
    )
    got = pl.pallas_call(
        body,
        out_shape=outs,
        in_specs=[IN_VMEM] * len(args),
        out_specs=[IN_VMEM] * len(outs),
        compiler_params=pltpu.CompilerParams(vmem_limit_bytes=VMEM_BYTES),
        cost_estimate=pl.CostEstimate(flops=1, bytes_accessed=1, transcendentals=0),
    )(*args)
    prepared = [tuple(got[i : i + 2]) for i in range(results, len(got), 2)]
    return list(got[:results]) + prepared


def by_core(values, offsets, n_dom, n_ref):
    pairs = [
        (d * n_ref + r, (d ^ offsets[r % 2]) * n_ref + r) for d in range(n_dom) for r in range(n_ref)
    ]
    return lax.ppermute(values, ("dom", "ref"), pairs)


def gather_plan(particles, references):
    n_ref = lax.axis_size("ref")
    n_dom = lax.axis_size("dom")
    block_rows = particles.shape[0]
    rows = block_rows // n_ref
    for_p = 1.0 / (block_rows * n_dom)
    for_r = -1.0 / (references.shape[0] * n_ref)
    place = lax.axis_index("ref")

    across = exchange(references, "ref", 3)
    near = by_core(particles, (2, 3), n_dom, n_ref)
    far = by_core(particles, (6, 7), n_dom, n_ref)
    middle = by_core(particles, (4, 5), n_dom, n_ref)
    mate = exchange(references, "ref", 1)

    near_sum, mate_pair = pull(near, [(for_r, [mate], [])])
    near_sum, mine, half, start_rows, own_pair = pull(
        near, [(for_r, [references], [])], near_sum, cut=particles
    )
    at_hand = [mate_pair, own_pair]
    beside = exchange(half, "dom", 1)
    far_sum = pull(after(far, near_sum), [(for_r, [], at_hand)])[0]
    fourth = jnp.concatenate([mine, after(beside, far_sum)])
    fourth_sum = pull(fourth, [(for_r, [], at_hand)])[0]
    middle = after(middle, fourth_sum)
    middle_sum = pull(middle, [(for_r, [], at_hand)])[0]

    held = jnp.concatenate([near, far, fourth, middle])
    held_sum = jnp.concatenate([near_sum, far_sum, fourth_sum, middle_sum])
    held_by_mate = exchange(held, "ref", 1)
    across = after(across, middle_sum)
    across_mate = exchange(across, "ref", 1)
    held_sum, across_pair = pull(held, [(for_r, [across], [])], held_sum)
    groups = [(for_p, [held, held_by_mate], []), (for_r, [across_mate], [])]
    moved, _, across_mate_pair = pull(held, groups, held_sum, moves=True)

    moved_by_mate = exchange(moved, "ref", 1)
    own_rows = lax.dynamic_slice_in_dim(moved, 2 * block_rows + (place // 2) * rows, rows, 0)
    groups = [(for_r, [], at_hand + [across_pair, across_mate_pair])]
    own_sum, moved_pair = pull(own_rows, groups, prepares=moved)
    groups = [(for_p, [moved_by_mate], [moved_pair])]
    return tuple(pull(own_rows, groups, own_sum, moves=True, start=start_rows)[:2])


def on_device(particles, references):
    if (lax.axis_size("dom"), lax.axis_size("ref")) == (8, 4) and STEPS == 2:
        return gather_plan(particles, references)
    return exchange_plan(particles, references)


def solution(mesh):
    placed = (P("dom", None), P("ref", None))
    return jax.shard_map(
        on_device,
        mesh=mesh,
        in_specs=placed,
        out_specs=(P(("dom", "ref"), None), P(("dom", "ref"), None)),
        check_vma=False,
    )
```

```python
import functools

import jax
import jax.numpy as jnp
from jax import lax
from jax.experimental import pallas as pl
from jax.experimental.pallas import tpu as pltpu
from jax.sharding import PartitionSpec as P

STEPS = 2


step_size = 0.5
LOG2E = 1.4426950408889634
TILE = 2048
VMEM_BYTES = 48 << 20
OVER_WIDTH = (((1,), (1,)), ((), ()))
IN_VMEM = pl.BlockSpec(memory_space=pltpu.VMEM)


def split(values):
    high = values.astype(jnp.bfloat16)
    return high, (values - high.astype(jnp.float32)).astype(jnp.bfloat16)


def half_square(values):
    return jnp.sum(values * values, axis=1, keepdims=True) * (-0.5 * LOG2E)


def left_operand(block):
    high, low = split(block * LOG2E)
    return jnp.concatenate(
        [jnp.concatenate([high, high], axis=1), jnp.concatenate([low, low], axis=1)], axis=0
    )


def prepare(others):
    return jnp.concatenate(split(others), axis=1), jnp.transpose(half_square(others))


def kernel_terms(left, left_square, right, square):
    rows = left.shape[0] // 2
    width = right.shape[1] // 2
    both = lax.dot_general(left, right, OVER_WIDTH, preferred_element_type=jnp.float32)
    weights = jnp.exp2(both[:rows] + both[rows:] + (left_square + square))
    pulled = jnp.dot(
        jnp.concatenate(split(weights), axis=0), right, preferred_element_type=jnp.float32
    )
    pulled = pulled[:rows] + pulled[rows:]
    return pulled[:, :width] + pulled[:, width:], jnp.sum(weights, axis=1, keepdims=True)


def all_terms(block, pieces):
    left = left_operand(block)
    left_square = half_square(block)
    pulled = jnp.zeros(block.shape, jnp.float32)
    summed = jnp.zeros((block.shape[0], 1), jnp.float32)
    for right, square in pieces:
        count = right.shape[0]
        for start in range(0, count, TILE):
            tile = slice(start, min(start + TILE, count))
            more = kernel_terms(left, left_square, right[tile, :], square[:, tile])
            pulled, summed = pulled + more[0], summed + more[1]
    return pulled - summed * block


def joined(refs):
    return jnp.concatenate([ref[...] for ref in refs], axis=0) if len(refs) > 1 else refs[0][...]


def own_slice(ref, rows):
    return ref[pl.ds(pl.multiple_of(lax.axis_index("ref") * rows, rows), rows), :]


def f32(*shape):
    return jax.ShapeDtypeStruct(shape, jnp.float32)


def exchange(values, axis, offset):
    size = lax.axis_size(axis)
    return lax.ppermute(values, axis, [(i, i ^ offset) for i in range(size)])


def after(values, *earlier):
    return lax.optimization_barrier((values,) + earlier)[0]


def references_kernel(count_r, block_ref, others_ref, out_ref, own_ref):
    block = block_ref[...]
    out_ref[...] = all_terms(block, [prepare(others_ref[...])]) * (-1.0 / count_r)
    own_ref[...] = own_slice(block_ref, own_ref.shape[0])


def partners_kernel(count_p, block_ref, first_ref, *refs):
    other_refs, out_ref = refs[:-1], refs[-1]
    others = prepare(joined(other_refs))
    out_ref[...] = first_ref[...] + all_terms(block_ref[...], [others]) * (1.0 / count_p)


def on_vmem(body, rows, *args):
    return pl.pallas_call(
        body,
        out_shape=[f32(r, args[0].shape[1]) for r in rows],
        in_specs=[IN_VMEM] * len(args),
        out_specs=[IN_VMEM] * len(rows),
        compiler_params=pltpu.CompilerParams(vmem_limit_bytes=VMEM_BYTES),
        cost_estimate=pl.CostEstimate(
            flops=8 * rows[0] * args[1].shape[0] * args[0].shape[1],
            bytes_accessed=4 * sum(a.size for a in args),
            transcendentals=rows[0] * args[1].shape[0],
        ),
    )(*args)


def offsets_of(n_dom, n_ref):
    share = n_dom // n_ref
    return [
        [i * n_ref + (r if i % 2 == 0 else n_ref - 1 - r) for i in reversed(range(share))]
        for r in range(n_ref)
    ]


def partner_blocks(block, n_dom, n_ref):
    offsets = offsets_of(n_dom, n_ref)
    blocks = []
    for i in range(n_dom // n_ref):
        pairs = [
            (d * n_ref + r, (d ^ offsets[r][i]) * n_ref + r)
            for d in range(n_dom)
            for r in range(n_ref)
        ]
        blocks.append(lax.ppermute(block, ("dom", "ref"), pairs))
    return blocks


def exchange_plan(particles, references):
    n_ref = lax.axis_size("ref")
    n_dom = lax.axis_size("dom")
    block_rows = particles.shape[0]
    rows = block_rows // n_ref
    count_p = block_rows * n_dom
    count_r = references.shape[0] * n_ref
    place = lax.axis_index("ref")
    block = particles
    for step in range(STEPS):
        partners = partner_blocks(block, n_dom, n_ref)
        partial_value, own = on_vmem(
            functools.partial(references_kernel, count_r),
            [block_rows, rows],
            block,
            references,
        )
        if step == 0:
            start_rows = own
        (partial_value,) = on_vmem(
            functools.partial(partners_kernel, count_p), [block_rows], block, partial_value, *partners
        )
        if step + 1 < STEPS:
            offset = 1
            while offset < n_ref:
                partial_value = partial_value + exchange(partial_value, "ref", offset)
                offset *= 2
            block = block - step_size * partial_value
        else:
            total = lax.dynamic_slice_in_dim(partial_value, place * rows, rows, 0)
            for offset in range(1, n_ref):
                chunk = lax.dynamic_slice_in_dim(partial_value, (place ^ offset) * rows, rows, 0)
                total = total + exchange(chunk, "ref", offset)
            own_rows = own - step_size * total
    return (own_rows, (own_rows - start_rows) / step_size)


def pull_kernel(scales, counts, has_first, moves, last, cut, prepares, *refs):
    refs = list(refs)

    def take(count):
        return [refs.pop(0) for _ in range(count)]

    (rows_ref,) = take(1)
    groups = [(take(raw), [tuple(take(2)) for _ in range(pairs)]) for raw, pairs in counts]
    first_refs = take(has_first)
    start_refs = take(last)
    whole_refs = take(cut)
    prepare_refs = take(prepares)
    (out_ref,) = take(1)
    drift_refs = take(last)
    if cut:
        cut_block(whole_refs[0], *take(3))
    rows = rows_ref[...]
    total = first_refs[0][...] if has_first else jnp.zeros(rows.shape, jnp.float32)
    for scale, (raw, pairs) in zip(scales, groups):
        pieces = []
        if raw:
            pieces.append(prepare(joined(raw)))
            for ref, value in zip(take(2), pieces[0]):
                ref[...] = value
        pieces += [(right[...], square[...]) for right, square in pairs]
        total += all_terms(rows, pieces) * scale
    if prepares:
        for ref, value in zip(take(2), prepare(prepare_refs[0][...])):
            ref[...] = value
    if moves:
        total = rows - step_size * total
    out_ref[...] = total
    if last:
        drift_refs[0][...] = (total - start_refs[0][...]) / step_size


def cut_block(block_ref, mine_ref, half_ref, start_ref):
    place = lax.axis_index("ref")
    core = lax.rem(place, 2)
    rows, half = start_ref.shape[0], half_ref.shape[0]

    def part(start, count):
        return block_ref[pl.ds(pl.multiple_of(start, rows), count), :]

    for i in range(mine_ref.shape[0] // rows):
        mine_ref[pl.ds(i * rows, rows), :] = part((2 * i + core) * rows, rows)
    half_ref[...] = part((1 - core) * half, half)
    start_ref[...] = part(place * rows, rows)


def pull(rows, groups, first=None, moves=False, start=None, cut=None, prepares=None):
    count, width = rows.shape
    args, outs = [rows], [f32(count, width)]
    if start is not None:
        outs.append(f32(count, width))
    if cut is not None:
        half = cut.shape[0] // 2
        outs += [f32(half, width), f32(half, width), f32(cut.shape[0] // lax.axis_size("ref"), width)]
    results = len(outs)
    for _, raw, pairs in groups:
        args += list(raw) + [value for pair in pairs for value in pair]
        if raw:
            size = sum(r.shape[0] for r in raw)
            outs += [jax.ShapeDtypeStruct((size, 2 * width), jnp.bfloat16), f32(1, size)]
    if prepares is not None:
        size = prepares.shape[0]
        outs += [jax.ShapeDtypeStruct((size, 2 * width), jnp.bfloat16), f32(1, size)]
    args += [value for value in (first, start, cut, prepares) if value is not None]
    body = functools.partial(
        pull_kernel,
        [scale for scale, _, _ in groups],
        [(len(raw), len(pairs)) for _, raw, pairs in groups],
        int(first is not None),
        moves,
        int(start is not None),
        int(cut is not None),
        int(prepares is not None),
    )
    got = pl.pallas_call(
        body,
        out_shape=outs,
        in_specs=[IN_VMEM] * len(args),
        out_specs=[IN_VMEM] * len(outs),
        compiler_params=pltpu.CompilerParams(vmem_limit_bytes=VMEM_BYTES),
        cost_estimate=pl.CostEstimate(flops=1, bytes_accessed=1, transcendentals=0),
    )(*args)
    prepared = [tuple(got[i : i + 2]) for i in range(results, len(got), 2)]
    return list(got[:results]) + prepared


def by_core(values, offsets, n_dom, n_ref):
    pairs = [
        (d * n_ref + r, (d ^ offsets[r % 2]) * n_ref + r) for d in range(n_dom) for r in range(n_ref)
    ]
    return lax.ppermute(values, ("dom", "ref"), pairs)


def gather_plan(particles, references):
    n_ref = lax.axis_size("ref")
    n_dom = lax.axis_size("dom")
    block_rows = particles.shape[0]
    rows = block_rows // n_ref
    for_p = 1.0 / (block_rows * n_dom)
    for_r = -1.0 / (references.shape[0] * n_ref)
    place = lax.axis_index("ref")

    across = exchange(references, "ref", 3)
    near = by_core(particles, (2, 3), n_dom, n_ref)
    far = by_core(particles, (6, 7), n_dom, n_ref)
    middle = by_core(particles, (4, 5), n_dom, n_ref)
    mate = exchange(references, "ref", 1)

    near_sum, mate_pair = pull(near, [(for_r, [mate], [])])
    near_sum, mine, half, start_rows, own_pair = pull(
        near, [(for_r, [references], [])], near_sum, cut=particles
    )
    at_hand = [mate_pair, own_pair]
    beside_pairs = [
        (d * n_ref + r, (d ^ 1) * n_ref + (r ^ 1)) for d in range(n_dom) for r in range(n_ref)
    ]
    beside = lax.ppermute(half, ("dom", "ref"), beside_pairs)
    far_sum = pull(after(far, near_sum), [(for_r, [], at_hand)])[0]
    fourth = jnp.concatenate([mine, after(beside, far_sum)])
    fourth_sum = pull(fourth, [(for_r, [], at_hand)])[0]
    middle = after(middle, fourth_sum)
    middle_sum = pull(middle, [(for_r, [], at_hand)])[0]

    held = jnp.concatenate([near, far, fourth, middle])
    held_sum = jnp.concatenate([near_sum, far_sum, fourth_sum, middle_sum])
    held_by_mate = exchange(held, "ref", 1)
    across = after(across, middle_sum)
    across_mate = exchange(across, "ref", 1)
    held_sum, across_pair = pull(held, [(for_r, [across], [])], held_sum)
    groups = [(for_p, [held, held_by_mate], []), (for_r, [across_mate], [])]
    moved, _, across_mate_pair = pull(held, groups, held_sum, moves=True)

    moved_by_mate = exchange(moved, "ref", 1)
    own_rows = lax.dynamic_slice_in_dim(moved, 2 * block_rows + (place // 2) * rows, rows, 0)
    groups = [(for_r, [], at_hand + [across_pair, across_mate_pair])]
    own_sum, moved_pair = pull(own_rows, groups, prepares=moved)
    groups = [(for_p, [moved_by_mate], [moved_pair])]
    return tuple(pull(own_rows, groups, own_sum, moves=True, start=start_rows)[:2])


def on_device(particles, references):
    if (lax.axis_size("dom"), lax.axis_size("ref")) == (8, 4) and STEPS == 2:
        return gather_plan(particles, references)
    return exchange_plan(particles, references)


def solution(mesh):
    placed = (P("dom", None), P("ref", None))
    return jax.shard_map(
        on_device,
        mesh=mesh,
        in_specs=placed,
        out_specs=(P(("dom", "ref"), None), P(("dom", "ref"), None)),
        check_vma=False,
    )
```

```python
import functools

import jax
import jax.numpy as jnp
from jax import lax
from jax.experimental import pallas as pl
from jax.experimental.pallas import tpu as pltpu
from jax.sharding import PartitionSpec as P

STEPS = 2


step_size = 0.5
LOG2E = 1.4426950408889634
TILE = 2048
VMEM_BYTES = 48 << 20
OVER_WIDTH = (((1,), (1,)), ((), ()))
IN_VMEM = pl.BlockSpec(memory_space=pltpu.VMEM)


def split(values):
    high = values.astype(jnp.bfloat16)
    return high, (values - high.astype(jnp.float32)).astype(jnp.bfloat16)


def half_square(values):
    return jnp.sum(values * values, axis=1, keepdims=True) * (-0.5 * LOG2E)


def left_operand(block):
    high, low = split(block * LOG2E)
    return jnp.concatenate(
        [jnp.concatenate([high, high], axis=1), jnp.concatenate([low, low], axis=1)], axis=0
    )


def prepare(others):
    return jnp.concatenate(split(others), axis=1), jnp.transpose(half_square(others))


def kernel_terms(left, left_square, right, square):
    rows = left.shape[0] // 2
    width = right.shape[1] // 2
    both = lax.dot_general(left, right, OVER_WIDTH, preferred_element_type=jnp.float32)
    weights = jnp.exp2(both[:rows] + both[rows:] + (left_square + square))
    pulled = jnp.dot(
        jnp.concatenate(split(weights), axis=0), right, preferred_element_type=jnp.float32
    )
    pulled = pulled[:rows] + pulled[rows:]
    return pulled[:, :width] + pulled[:, width:], jnp.sum(weights, axis=1, keepdims=True)


def all_terms(block, pieces):
    left = left_operand(block)
    left_square = half_square(block)
    pulled = jnp.zeros(block.shape, jnp.float32)
    summed = jnp.zeros((block.shape[0], 1), jnp.float32)
    for right, square in pieces:
        count = right.shape[0]
        for start in range(0, count, TILE):
            tile = slice(start, min(start + TILE, count))
            more = kernel_terms(left, left_square, right[tile, :], square[:, tile])
            pulled, summed = pulled + more[0], summed + more[1]
    return pulled - summed * block


def joined(refs):
    return jnp.concatenate([ref[...] for ref in refs], axis=0) if len(refs) > 1 else refs[0][...]


def own_slice(ref, rows):
    return ref[pl.ds(pl.multiple_of(lax.axis_index("ref") * rows, rows), rows), :]


def f32(*shape):
    return jax.ShapeDtypeStruct(shape, jnp.float32)


def exchange(values, axis, offset):
    size = lax.axis_size(axis)
    return lax.ppermute(values, axis, [(i, i ^ offset) for i in range(size)])


def after(values, *earlier):
    return lax.optimization_barrier((values,) + earlier)[0]


def references_kernel(count_r, block_ref, others_ref, out_ref, own_ref):
    block = block_ref[...]
    out_ref[...] = all_terms(block, [prepare(others_ref[...])]) * (-1.0 / count_r)
    own_ref[...] = own_slice(block_ref, own_ref.shape[0])


def partners_kernel(count_p, block_ref, first_ref, *refs):
    other_refs, out_ref = refs[:-1], refs[-1]
    others = prepare(joined(other_refs))
    out_ref[...] = first_ref[...] + all_terms(block_ref[...], [others]) * (1.0 / count_p)


def on_vmem(body, rows, *args):
    return pl.pallas_call(
        body,
        out_shape=[f32(r, args[0].shape[1]) for r in rows],
        in_specs=[IN_VMEM] * len(args),
        out_specs=[IN_VMEM] * len(rows),
        compiler_params=pltpu.CompilerParams(vmem_limit_bytes=VMEM_BYTES),
        cost_estimate=pl.CostEstimate(
            flops=8 * rows[0] * args[1].shape[0] * args[0].shape[1],
            bytes_accessed=4 * sum(a.size for a in args),
            transcendentals=rows[0] * args[1].shape[0],
        ),
    )(*args)


def offsets_of(n_dom, n_ref):
    share = n_dom // n_ref
    return [
        [i * n_ref + (r if i % 2 == 0 else n_ref - 1 - r) for i in reversed(range(share))]
        for r in range(n_ref)
    ]


def partner_blocks(block, n_dom, n_ref):
    offsets = offsets_of(n_dom, n_ref)
    blocks = []
    for i in range(n_dom // n_ref):
        pairs = [
            (d * n_ref + r, (d ^ offsets[r][i]) * n_ref + r)
            for d in range(n_dom)
            for r in range(n_ref)
        ]
        blocks.append(lax.ppermute(block, ("dom", "ref"), pairs))
    return blocks


def exchange_plan(particles, references):
    n_ref = lax.axis_size("ref")
    n_dom = lax.axis_size("dom")
    block_rows = particles.shape[0]
    rows = block_rows // n_ref
    count_p = block_rows * n_dom
    count_r = references.shape[0] * n_ref
    place = lax.axis_index("ref")
    block = particles
    for step in range(STEPS):
        partners = partner_blocks(block, n_dom, n_ref)
        partial_value, own = on_vmem(
            functools.partial(references_kernel, count_r),
            [block_rows, rows],
            block,
            references,
        )
        if step == 0:
            start_rows = own
        (partial_value,) = on_vmem(
            functools.partial(partners_kernel, count_p), [block_rows], block, partial_value, *partners
        )
        if step + 1 < STEPS:
            offset = 1
            while offset < n_ref:
                partial_value = partial_value + exchange(partial_value, "ref", offset)
                offset *= 2
            block = block - step_size * partial_value
        else:
            total = lax.dynamic_slice_in_dim(partial_value, place * rows, rows, 0)
            for offset in range(1, n_ref):
                chunk = lax.dynamic_slice_in_dim(partial_value, (place ^ offset) * rows, rows, 0)
                total = total + exchange(chunk, "ref", offset)
            own_rows = own - step_size * total
    return (own_rows, (own_rows - start_rows) / step_size)


def pull_kernel(scales, counts, has_first, moves, last, cut, prepares, *refs):
    refs = list(refs)

    def take(count):
        return [refs.pop(0) for _ in range(count)]

    (rows_ref,) = take(1)
    groups = [(take(raw), [tuple(take(2)) for _ in range(pairs)]) for raw, pairs in counts]
    first_refs = take(has_first)
    start_refs = take(last)
    whole_refs = take(cut)
    prepare_refs = take(prepares)
    (out_ref,) = take(1)
    drift_refs = take(last)
    if cut:
        cut_block(whole_refs[0], *take(3))
    rows = rows_ref[...]
    total = first_refs[0][...] if has_first else jnp.zeros(rows.shape, jnp.float32)
    for scale, (raw, pairs) in zip(scales, groups):
        pieces = []
        if raw:
            pieces.append(prepare(joined(raw)))
            for ref, value in zip(take(2), pieces[0]):
                ref[...] = value
        pieces += [(right[...], square[...]) for right, square in pairs]
        total += all_terms(rows, pieces) * scale
    if prepares:
        for ref, value in zip(take(2), prepare(prepare_refs[0][...])):
            ref[...] = value
    if moves:
        total = rows - step_size * total
    out_ref[...] = total
    if last:
        drift_refs[0][...] = (total - start_refs[0][...]) / step_size


def cut_block(block_ref, mine_ref, half_ref, start_ref):
    place = lax.axis_index("ref")
    core = lax.rem(place, 2)
    rows, half = start_ref.shape[0], half_ref.shape[0]

    def part(start, count):
        return block_ref[pl.ds(pl.multiple_of(start, rows), count), :]

    for i in range(mine_ref.shape[0] // rows):
        mine_ref[pl.ds(i * rows, rows), :] = part((2 * i + core) * rows, rows)
    half_ref[...] = part((1 - core) * half, half)
    start_ref[...] = part(place * rows, rows)


def pull(rows, groups, first=None, moves=False, start=None, cut=None, prepares=None):
    count, width = rows.shape
    args, outs = [rows], [f32(count, width)]
    if start is not None:
        outs.append(f32(count, width))
    if cut is not None:
        half = cut.shape[0] // 2
        outs += [f32(half, width), f32(half, width), f32(cut.shape[0] // lax.axis_size("ref"), width)]
    results = len(outs)
    for _, raw, pairs in groups:
        args += list(raw) + [value for pair in pairs for value in pair]
        if raw:
            size = sum(r.shape[0] for r in raw)
            outs += [jax.ShapeDtypeStruct((size, 2 * width), jnp.bfloat16), f32(1, size)]
    if prepares is not None:
        size = prepares.shape[0]
        outs += [jax.ShapeDtypeStruct((size, 2 * width), jnp.bfloat16), f32(1, size)]
    args += [value for value in (first, start, cut, prepares) if value is not None]
    body = functools.partial(
        pull_kernel,
        [scale for scale, _, _ in groups],
        [(len(raw), len(pairs)) for _, raw, pairs in groups],
        int(first is not None),
        moves,
        int(start is not None),
        int(cut is not None),
        int(prepares is not None),
    )
    got = pl.pallas_call(
        body,
        out_shape=outs,
        in_specs=[IN_VMEM] * len(args),
        out_specs=[IN_VMEM] * len(outs),
        compiler_params=pltpu.CompilerParams(vmem_limit_bytes=VMEM_BYTES),
        cost_estimate=pl.CostEstimate(flops=1, bytes_accessed=1, transcendentals=0),
    )(*args)
    prepared = [tuple(got[i : i + 2]) for i in range(results, len(got), 2)]
    return list(got[:results]) + prepared


def by_core(values, offsets, n_dom, n_ref):
    pairs = [
        (d * n_ref + r, (d ^ offsets[r % 2]) * n_ref + r) for d in range(n_dom) for r in range(n_ref)
    ]
    return lax.ppermute(values, ("dom", "ref"), pairs)


def gather_plan(particles, references):
    n_ref = lax.axis_size("ref")
    n_dom = lax.axis_size("dom")
    block_rows = particles.shape[0]
    rows = block_rows // n_ref
    for_p = 1.0 / (block_rows * n_dom)
    for_r = -1.0 / (references.shape[0] * n_ref)
    place = lax.axis_index("ref")

    across = exchange(references, "ref", 3)
    near = by_core(particles, (2, 3), n_dom, n_ref)
    far = by_core(particles, (6, 7), n_dom, n_ref)
    middle = by_core(particles, (4, 5), n_dom, n_ref)
    mate = exchange(references, "ref", 1)

    near_sum, mate_pair = pull(near, [(for_r, [mate], [])])
    near_sum, mine, half, start_rows, own_pair = pull(
        near, [(for_r, [references], [])], near_sum, cut=particles
    )
    at_hand = [mate_pair, own_pair]
    beside_pairs = [
        (d * n_ref + r, (d ^ 1) * n_ref + (r ^ 1)) for d in range(n_dom) for r in range(n_ref)
    ]
    beside = lax.ppermute(half, ("dom", "ref"), beside_pairs)
    far_sum = pull(after(far, near_sum), [(for_r, [], at_hand)])[0]
    fourth = jnp.concatenate([mine, after(beside, far_sum)])
    fourth_sum = pull(fourth, [(for_r, [], at_hand)])[0]
    middle = after(middle, fourth_sum)
    middle_sum = pull(middle, [(for_r, [], at_hand)])[0]

    held = jnp.concatenate([near, far, fourth, middle])
    held_sum = jnp.concatenate([near_sum, far_sum, fourth_sum, middle_sum])
    held_by_mate = exchange(held, "ref", 1)
    across = after(across, middle_sum)
    across_mate = exchange(across, "ref", 1)
    held_sum, across_pair = pull(held, [(for_r, [across], [])], held_sum)
    groups = [(for_r, [across_mate], []), (for_p, [held, held_by_mate], [])]
    moved, across_mate_pair, _ = pull(held, groups, held_sum, moves=True)

    moved_by_mate = exchange(moved, "ref", 1)
    own_rows = lax.dynamic_slice_in_dim(moved, 2 * block_rows + (place // 2) * rows, rows, 0)
    groups = [(for_r, [], at_hand + [across_pair, across_mate_pair])]
    own_sum, moved_pair = pull(own_rows, groups, prepares=moved)
    groups = [(for_p, [moved_by_mate], [moved_pair])]
    return tuple(pull(own_rows, groups, own_sum, moves=True, start=start_rows)[:2])


def on_device(particles, references):
    if (lax.axis_size("dom"), lax.axis_size("ref")) == (8, 4) and STEPS == 2:
        return gather_plan(particles, references)
    return exchange_plan(particles, references)


def solution(mesh):
    placed = (P("dom", None), P("ref", None))
    return jax.shard_map(
        on_device,
        mesh=mesh,
        in_specs=placed,
        out_specs=(P(("dom", "ref"), None), P(("dom", "ref"), None)),
        check_vma=False,
    )
```
